32 devices in a mesh: slab: 4 (over z), brick: 8 (over y, x, core).
Axes of the slice: x: 2, y: 2, z: 4, core: 2. Of those that a mesh axis runs over, the one named last changes fastest.
Arguments:
- estimate: float32 [32, 512, 128], P('slab', 'brick'), may hold values from 0.5 to 2
- stored_data: float32 [8, 8, 6, 32, 16, 128], P('brick', None, None, 'slab'), may hold values from 0.5 to 2
- routes: int32 [8, 24], replicated, may hold values from 0 to 7, as said below
- offsets: int32 [6, 32], replicated, may hold values from -2 to 2
- depth_taps: float32 [6, 9], replicated, may hold values from 0.1 to 1
- row_taps: float32 [6, 5], replicated, may hold values from 0.1 to 1
- column_taps: float32 [6, 9], replicated, may hold values from 0.1 to 1
- background: float32 [6], replicated, may hold values from 0.2 to 0.6
Outputs:
- restored: float32 [32, 512, 128], P('slab', 'brick')
The draws below stay inside these ranges and needn't reach their ends.
Inputs may be any that keep to these rules, and one draw needn't show every extreme that they name: routes[b, q] is the owner of block q % 4 of view q // 4 within device b's y-rows; an owner holds at most 6 blocks of one device's rows, and 2 owners hold 6 blocks of every device's rows.
All inputs are finite; a program needn't handle non-finite values.
Results may differ from the reference program's by a relative error of at most 0.00031.
Values may be sent and summed in bfloat16 or wider, within the bound.
A program may use at most 128 MiB of HBM per device.

```python
import math
import jax
import jax.numpy as jnp
from jax import lax

V = 6
CX = 128
BY = 16
KB = 4
W = 4
RY = 2
RX = 4
ITERS = 2
NB = 8
NY = 512
NZ = 32
NBLK = 32
CAP = 6
NBUSY = 2
N_BRICK = 8


def draw_routes(key, part):
    first_key, second_key, third_key = jax.random.split(key, 3)
    token_count = NB * CAP
    block_count = V * KB
    shuffled = jax.random.permutation(first_key, NB)
    ranking = jnp.zeros((NB,), jnp.int32).at[shuffled].set(jnp.arange(NB, dtype=jnp.int32))
    busy_flag = (ranking < NBUSY).astype(jnp.int32)
    token_owner = jnp.arange(token_count, dtype=jnp.int32) // CAP
    noise = jax.random.randint(second_key, (NB, token_count), 0, 4096)
    scores = (busy_flag[token_owner][None, :] * 4096 + noise) * token_count + jnp.arange(token_count, dtype=jnp.int32)[None, :]
    chosen = lax.top_k(scores, block_count)[1]
    owners = (chosen // CAP).astype(jnp.int32)
    mixing = jax.random.randint(third_key, (NB, block_count), 0, 4096) * block_count + jnp.arange(block_count, dtype=jnp.int32)[None, :]
    ordering = jnp.argsort(mixing, axis=1)
    return jnp.take_along_axis(owners, ordering, axis=1).astype(jnp.int32)


def touch_ends(result, key, low, high):
    spot = [jax.random.randint(jax.random.fold_in(key, axis), (), 0, length) for axis, length in enumerate(result.shape)]
    longest = result.shape.index(max(result.shape))
    neighbour = spot[:longest] + [(spot[longest] + 1) % result.shape[longest]] + spot[longest + 1:]
    return result.at[tuple(spot)].set(low).at[tuple(neighbour)].set(high)


def block_scale(rng, extent, shards, smallest, high):
    gain = 1.0
    for dim, shards_of in shards:
        heights = jax.random.uniform(jax.random.fold_in(jax.random.fold_in(rng, 6), dim), (shards_of,), jnp.float32, smallest / len(shards), high / len(shards))
        gain = gain * jnp.repeat(jnp.exp(heights), extent[dim] // shards_of).reshape((-1,) + (1,) * (len(extent) - 1 - dim))
    return gain


def setup_inputs(seed: int = 0) -> dict:
    splits = jax.random.split(jax.random.key(seed), 9)
    return {
        "estimate": jnp.clip(jnp.exp(math.log(2.0) - 1.3862944 * jax.random.uniform(splits[0], (NZ, NY, CX), jnp.float32) ** block_scale(splits[0], (NZ, NY, CX), ((0, 4), (1, 8)), -0.2, 0.2)), 0.5, 2.0),
        "stored_data": jnp.clip(jnp.exp(math.log(2.0) - 1.3862944 * jax.random.uniform(splits[1], (N_BRICK, N_BRICK, CAP, NZ, BY, CX), jnp.float32) ** block_scale(splits[1], (N_BRICK, N_BRICK, CAP, NZ, BY, CX), ((0, 8), (3, 4)), -0.2, 0.2)), 0.5, 2.0),
        "routes": draw_routes(jax.random.fold_in(splits[8], 71), 0),
        "offsets": touch_ends(jax.random.randint(splits[3], (V, NBLK), RY - W, W - RY + 1), jax.random.fold_in(splits[3], 1), RY - W, W - RY).astype(jnp.int32),
        "depth_taps": jnp.clip(jnp.exp(jax.random.uniform(splits[4], (V, 2 * W + 1), jnp.float32, math.log(0.1), math.log(1.0))), 0.1, 1.0),
        "row_taps": jnp.clip(jnp.exp(jax.random.uniform(splits[5], (V, 2 * RY + 1), jnp.float32, math.log(0.1), math.log(1.0))), 0.1, 1.0),
        "column_taps": jnp.clip(jnp.exp(jax.random.uniform(splits[6], (V, 2 * RX + 1), jnp.float32, math.log(0.1), math.log(1.0))), 0.1, 1.0),
        "background": jnp.clip(jnp.exp(jax.random.uniform(splits[7], (V,), jnp.float32, math.log(0.2), math.log(0.6))), 0.2, 0.6),
    }


def normalized(taps):
    return taps / jnp.sum(taps, axis=-1, keepdims=True)


def cross_matrix(column_kernel):
    row_index = jnp.arange(CX, dtype=jnp.int32)[:, None]
    col_index = jnp.arange(CX, dtype=jnp.int32)[None, :]
    lag_index = row_index - col_index + RX
    summed = jnp.zeros(column_kernel.shape[:-1] + (CX, CX), jnp.float32)
    for position in range(2 * RX + 1):
        summed = summed + column_kernel[..., position, None, None] * (lag_index == position).astype(jnp.float32)
    return summed.astype(jnp.bfloat16)


def slot_numbers(routes):
    width_count = routes.shape[1]
    same_owner = routes[:, :, None] == routes[:, None, :]
    earlier = jnp.arange(width_count, dtype=jnp.int32)[None, :] < jnp.arange(width_count, dtype=jnp.int32)[:, None]
    return jnp.sum((same_owner & earlier[None]).astype(jnp.int32), axis=2).astype(jnp.int32)


def reference(estimate, stored_data, routes, offsets, depth_taps, row_taps, column_taps, background):
    kernel_z = normalized(depth_taps)
    kernel_y = normalized(row_taps)
    kernel_x = normalized(column_taps)
    slots = slot_numbers(routes)
    source = jnp.broadcast_to(jnp.arange(NB, dtype=jnp.int32)[:, None], routes.shape)
    recorded = stored_data[routes, source, slots]
    recorded = recorded.reshape(NB, V, KB, NZ, BY, CX).transpose(1, 3, 0, 2, 4, 5).reshape(V, NZ, NY, CX)
    shift_room = W - RY
    for sweep in range(ITERS):
        rounded = estimate.astype(jnp.bfloat16)
        padded = jnp.pad(rounded, ((W, W), (W, W), (0, 0)))
        summed = jnp.zeros((NZ, NY, CX), jnp.float32)
        for view in range(V):
            matrix = cross_matrix(kernel_x[view])
            across = jnp.dot(padded.reshape(-1, CX), matrix, preferred_element_type=jnp.float32)
            across = across.reshape(NZ + 2 * W, NY + 2 * W, CX)
            row_blur = jnp.zeros((NZ + 2 * W, NY + 2 * shift_room, CX), jnp.float32)
            for position in range(2 * RY + 1):
                row_blur = row_blur + kernel_y[view, position] * across[:, position:position + NY + 2 * shift_room]
            depth_blur = jnp.zeros((NZ, NY + 2 * shift_room, CX), jnp.float32)
            for position in range(2 * W + 1):
                depth_blur = depth_blur + kernel_z[view, position] * row_blur[position:position + NZ]
            row_index = (jnp.arange(NY, dtype=jnp.int32) + jnp.repeat(offsets[view], BY) + shift_room).astype(jnp.int32)
            blurred = jnp.take(depth_blur, row_index, axis=1)
            ratio = recorded[view] / (background[view] + blurred)
            backward = jnp.dot(ratio.astype(jnp.bfloat16).reshape(-1, CX), matrix.T, preferred_element_type=jnp.float32)
            backward = backward.reshape(NZ, NY, CX)
            spread = jnp.zeros((NZ, NY + 2 * shift_room, CX), jnp.float32).at[:, row_index].add(backward)
            spread = jnp.pad(spread, ((0, 0), (RY, RY), (0, 0)))
            row_back = jnp.zeros((NZ, NY, CX), jnp.float32)
            for position in range(2 * RY + 1):
                first_row = shift_room + 2 * RY - position
                row_back = row_back + kernel_y[view, position] * spread[:, first_row:first_row + NY]
            row_back = jnp.pad(row_back, ((W, W), (0, 0), (0, 0)))
            for position in range(2 * W + 1):
                first_depth = 2 * W - position
                summed = summed + kernel_z[view, position] * row_back[first_depth:first_depth + NZ]
        estimate = estimate * (summed / V)
    return estimate
```

```python
import functools

import jax
import jax.numpy as jnp
from jax import lax
from jax.experimental import pallas as pl
from jax.experimental.pallas import tpu as pltpu
from jax.sharding import PartitionSpec as P

V = 6
CX = 128
BY = 16
KB = 4
W = 4
RY = 2
RX = 4
ITERS = 2
TZ = 2 * W + 1
TY = 2 * RY + 1
TX = 2 * RX + 1
MIDDLE = 1.25
SCALE = 43680.0
DIRECTIONS = [(dz, db) for dz in (-1, 0, 1) for db in (-1, 0, 1) if (dz, db) != (0, 0)]
MESH = pl.DeviceIdType.MESH


def kernel(
    slabs,
    bricks,
    routes,
    offsets,
    depth_taps,
    row_taps,
    column_taps,
    background,
    estimate,
    stored,
    restored,
    staged,
    coded,
    received,
    slots,
    rounded,
    extended,
    zblur,
    back,
    spread,
    correction,
    total,
    forward,
    backward,
    scales,
    halos,
    returns,
    load_sem,
    data_send,
    data_recv,
    halo_send,
    halo_recv,
    return_send,
    return_recv,
):
    slab = lax.axis_index("slab")
    brick = lax.axis_index("brick")
    capacity = stored.shape[1]
    depth, height, _ = estimate.shape
    padded = height + 2 * W
    tiles = padded // 8

    def load_copy(target):
        return pltpu.make_async_copy(stored.at[target], staged.at[target], load_sem.at[target])

    for step in range(bricks):
        load_copy(lax.rem(brick + step, bricks)).start()

    def present(dz, db):
        there_slab = slab + dz
        there_brick = brick + db
        return (
            (there_slab >= 0) & (there_slab < slabs) & (there_brick >= 0) & (there_brick < bricks)
        )

    for buffer in tuple(halos) + tuple(returns):
        buffer[...] = jnp.zeros_like(buffer)

    barrier = pltpu.get_barrier_semaphore()
    for step in range(1, bricks):
        pl.semaphore_signal(
            barrier,
            inc=1,
            device_id=(slab, lax.rem(brick + step, bricks)),
            device_id_type=MESH,
        )
    expected = jnp.int32(bricks - 1)
    for dz, db in DIRECTIONS:
        if dz == 0:
            continue

        @pl.when(present(dz, db))
        def _():
            pl.semaphore_signal(
                barrier, inc=1, device_id=(slab + dz, brick + db), device_id_type=MESH
            )

        expected = expected + present(dz, db).astype(jnp.int32)
    estimate_now = estimate[...]
    rounded[0] = estimate_now.astype(jnp.bfloat16)
    pl.semaphore_wait(barrier, expected)

    def halo_copy(sweep, index):
        dz, db = DIRECTIONS[index]
        planes = {-1: pl.ds(0, W), 0: pl.ds(0, depth), 1: pl.ds(depth - W, W)}[dz]
        rows = {-1: pl.ds(0, 16), 0: pl.ds(0, height), 1: pl.ds(height - 16, 16)}[db]
        return pltpu.make_async_remote_copy(
            src_ref=rounded.at[sweep, planes, rows],
            dst_ref=halos[index].at[sweep],
            send_sem=halo_send.at[sweep, index],
            recv_sem=halo_recv.at[sweep, index],
            device_id=(slab + dz, brick + db),
            device_id_type=MESH,
        )

    def return_copy(sweep, index):
        dz, db = DIRECTIONS[index]
        planes = {-1: pl.ds(0, W), 0: pl.ds(W, depth), 1: pl.ds(depth + W, W)}[dz]
        rows = {-1: pl.ds(0, 8), 0: pl.ds(0, padded), 1: pl.ds(padded - 8, 8)}[db]
        return pltpu.make_async_remote_copy(
            src_ref=correction.at[sweep, planes, rows],
            dst_ref=returns[index].at[sweep],
            send_sem=return_send.at[sweep, index],
            recv_sem=return_recv.at[sweep, index],
            device_id=(slab + dz, brick + db),
            device_id_type=MESH,
        )

    def send_all(copy, sweep):
        for index, (dz, db) in enumerate(DIRECTIONS):

            @pl.when(present(dz, db))
            def _():
                copy(sweep, index).start()

    def receive_all(copy, sweep):
        for index, (dz, db) in enumerate(DIRECTIONS):

            @pl.when(present(-dz, -db))
            def _():
                copy(sweep, index).wait_recv()

    def sent_all(copy, sweep):
        for index, (dz, db) in enumerate(DIRECTIONS):

            @pl.when(present(dz, db))
            def _():
                copy(sweep, index).wait_send()

    def data_copy(target, source):
        return pltpu.make_async_remote_copy(
            src_ref=coded.at[target],
            dst_ref=received.at[brick],
            send_sem=data_send.at[target],
            recv_sem=data_recv.at[source],
            device_id=(slab, target),
            device_id_type=MESH,
        )

    def encode(cells):
        return jnp.round((cells - MIDDLE) * SCALE).astype(jnp.int32).astype(jnp.int16)

    send_all(halo_copy, 0)

    def send_step(step, carry):
        target = lax.rem(brick + step, bricks)
        load_copy(target).wait()

        def code_slot(slot, inner):
            coded[target, slot] = encode(staged[target, slot])
            return inner

        lax.fori_loop(0, capacity, code_slot, 0)
        data_copy(target, brick).start()
        return carry

    lax.fori_loop(1, bricks, send_step, 0)
    load_copy(brick).wait()

    def code_own(slot, carry):
        received[brick, slot] = encode(staged[brick, slot])
        return carry

    lax.fori_loop(0, capacity, code_own, 0)

    def number_slots(position, carry):
        owner = routes[brick, position]
        count = jnp.int32(0)
        for other in range(V * KB):
            same = (routes[brick, other] == owner) & (other < position)
            count = count + jnp.where(same, 1, 0)
        slots[position] = jnp.minimum(count, capacity - 1)
        return carry

    lax.fori_loop(0, V * KB, number_slots, 0)

    row_index = lax.broadcasted_iota(jnp.int32, (CX, CX), 0)
    col_index = lax.broadcasted_iota(jnp.int32, (CX, CX), 1)

    def build_view(view, carry):
        sum_x = column_taps[view, 0]
        for position in range(1, TX):
            sum_x = sum_x + column_taps[view, position]
        sum_y = row_taps[view, 0]
        for position in range(1, TY):
            sum_y = sum_y + row_taps[view, position]
        sum_z = depth_taps[view, 0]
        for position in range(1, TZ):
            sum_z = sum_z + depth_taps[view, position]
        ones = jnp.ones((8, CX), jnp.float32)
        scales[view] = ones / (ones * (sum_y * sum_z))
        lag = row_index - col_index + RX
        matrix = jnp.zeros((CX, CX), jnp.float32)
        flipped = jnp.zeros((CX, CX), jnp.float32)
        bottom = jnp.full((1, CX), sum_x, jnp.float32)
        for position in range(TX):
            tap = jnp.full((1, CX), column_taps[view, position], jnp.float32) / bottom
            matrix = jnp.where(lag == position, tap, matrix)
            flipped = jnp.where(lag == 2 * RX - position, tap, flipped)
        matrix = matrix.astype(jnp.bfloat16)
        forward[view, 0:CX] = matrix
        forward[view, CX : 2 * CX] = matrix
        backward[view] = flipped.astype(jnp.bfloat16)
        return carry

    lax.fori_loop(0, V, build_view, 0)

    def clear(position, carry):
        back[position, :, 0:8] = jnp.zeros((depth, 8, CX), jnp.float32)
        back[position, :, 8 + BY : 16 + BY] = jnp.zeros((depth, 8, CX), jnp.float32)
        return carry

    lax.fori_loop(0, V * KB, clear, 0)

    for sweep in range(ITERS):
        if sweep > 0:
            rounded[sweep] = estimate_now.astype(jnp.bfloat16)
            send_all(halo_copy, sweep)
        extended[W : W + depth, W : W + height] = rounded[sweep].astype(jnp.float32)
        receive_all(halo_copy, sweep)
        for index, (dz, db) in enumerate(DIRECTIONS):
            planes = {1: (0, W), 0: (W, W + depth), -1: (W + depth, 2 * W + depth)}[dz]
            rows = {1: (0, W), 0: (W, W + height), -1: (W + height, padded)}[db]
            taken = {1: (16 - W, 16), 0: (0, height), -1: (0, W)}[db]
            block = halos[index][sweep].astype(jnp.float32)
            extended[planes[0] : planes[1], rows[0] : rows[1]] = block[:, taken[0] : taken[1]]

        def blur_tile(tile, carry):
            start = pl.multiple_of(tile * 8, 8)
            planes = [extended[z, pl.ds(start, 8)] for z in range(depth + 2 * W)]
            for view in range(V):
                taps = [depth_taps[view, position] for position in range(TZ)]
                for z in range(depth):
                    value = taps[0] * planes[z]
                    for position in range(1, TZ):
                        value = value + taps[position] * planes[z + position]
                    zblur[view, z, pl.ds(start, 8)] = value
            return carry

        lax.fori_loop(0, tiles, blur_tile, 0)

        if sweep == 0:

            def receive_step(step, carry):
                source = lax.rem(brick + step, bricks)
                data_copy(source, source).wait_recv()
                return carry

            lax.fori_loop(1, bricks, receive_step, 0)

        def block_step(position, carry):
            view = position // KB
            piece = position % KB
            shift = offsets[view, brick * KB + piece]
            first = piece * BY + W - RY + shift
            blurred = row_taps[view, 0] * zblur[view, :, pl.ds(first, BY)]
            for tap in range(1, TY):
                blurred = blurred + row_taps[view, tap] * zblur[view, :, pl.ds(first + tap, BY)]
            blurred = blurred.reshape(depth * BY, CX)
            high = blurred.astype(jnp.bfloat16)
            low = (blurred - high.astype(jnp.float32)).astype(jnp.bfloat16)
            factor = scales[view, 0:1]
            blurred = factor * jnp.dot(
                jnp.concatenate([high, low], axis=1),
                forward[view],
                preferred_element_type=jnp.float32,
            )
            code = received[routes[brick, position], slots[position]].astype(jnp.int32)
            data = code.astype(jnp.float32) * (1.0 / SCALE) + MIDDLE
            ratio = data.reshape(depth * BY, CX) / (background[view] + blurred)
            result = factor * jnp.dot(
                ratio.astype(jnp.bfloat16), backward[view], preferred_element_type=jnp.float32
            )
            back[position, :, 8 : 8 + BY] = result.reshape(depth, BY, CX)
            return carry

        lax.fori_loop(0, V * KB, block_step, 0)

        def spread_view(view, carry):
            edge = None
            for piece in range(KB):
                position = view * KB + piece
                shift = offsets[view, brick * KB + piece]
                value = None
                for tap in range(TY):
                    term = row_taps[view, tap] * back[
                        position, :, pl.ds(W - shift - (tap - RY), BY + 2 * W)
                    ]
                    value = term if value is None else value + term
                top = value[:, 0:8]
                if edge is not None:
                    top = top + edge
                spread[view, :, piece * BY : piece * BY + 8] = top
                spread[view, :, piece * BY + 8 : piece * BY + 16] = value[:, 8:16]
                edge = value[:, 16:24]
            spread[view, :, KB * BY : KB * BY + 8] = edge
            return carry

        lax.fori_loop(0, V, spread_view, 0)

        def deep_tile(tile, carry):
            start = pl.multiple_of(tile * 8, 8)
            sums = [None] * (depth + 2 * W)
            for view in range(V):
                taps = [depth_taps[view, position] for position in range(TZ)]
                for z in range(depth):
                    plane = spread[view, z, pl.ds(start, 8)]
                    for position in range(TZ):
                        term = taps[position] * plane
                        old = sums[z + position]
                        sums[z + position] = term if old is None else old + term
            for z in range(depth + 2 * W):
                correction[sweep, z, pl.ds(start, 8)] = sums[z]
            return carry

        lax.fori_loop(0, tiles, deep_tile, 0)

        send_all(return_copy, sweep)
        total[...] = correction[sweep, W : W + depth, W : W + height]
        receive_all(return_copy, sweep)
        for index, (dz, db) in enumerate(DIRECTIONS):
            planes = {1: (0, W), 0: (0, depth), -1: (depth - W, depth)}[dz]
            rows = {1: (0, W), 0: (0, height), -1: (height - W, height)}[db]
            taken = {1: (8 - W, 8), 0: (W, W + height), -1: (0, W)}[db]
            total[planes[0] : planes[1], rows[0] : rows[1]] += returns[index][
                sweep, :, taken[0] : taken[1]
            ]
        if sweep + 1 < ITERS:
            estimate_now = estimate_now * (total[...] / V)
        else:
            restored[...] = estimate_now * (total[...] / V)

    for sweep in range(ITERS):
        sent_all(halo_copy, sweep)
        sent_all(return_copy, sweep)

    def sent_step(step, carry):
        data_copy(lax.rem(brick + step, bricks), brick).wait_send()
        return carry

    lax.fori_loop(1, bricks, sent_step, 0)


def local(slabs, bricks, estimate, stored_data, routes, offsets, depth_taps, row_taps, column_taps, background):
    depth, height, width = estimate.shape
    stored = stored_data.reshape(stored_data.shape[1:])
    capacity = stored.shape[1]
    padded = height + 2 * W
    halo_planes = {-1: W, 0: depth, 1: W}
    halo_rows = {-1: 16, 0: height, 1: 16}
    return_rows = {-1: 8, 0: padded, 1: 8}
    smem = pl.BlockSpec(memory_space=pltpu.SMEM)
    vmem = pl.BlockSpec(memory_space=pltpu.VMEM)
    count = len(DIRECTIONS)
    return pl.pallas_call(
        functools.partial(kernel, slabs, bricks),
        out_shape=jax.ShapeDtypeStruct((depth, height, width), jnp.float32),
        in_specs=[smem] * 6 + [vmem, pl.BlockSpec(memory_space=pl.ANY)],
        out_specs=vmem,
        scratch_shapes=[
            pltpu.VMEM((bricks, capacity, depth, BY, width), jnp.float32),
            pltpu.VMEM((bricks, capacity, depth, BY, width), jnp.int16),
            pltpu.VMEM((bricks, capacity, depth, BY, width), jnp.int16),
            pltpu.SMEM((V * KB,), jnp.int32),
            pltpu.VMEM((ITERS, depth, height, width), jnp.bfloat16),
            pltpu.VMEM((depth + 2 * W, padded, width), jnp.float32),
            pltpu.VMEM((V, depth, padded, width), jnp.float32),
            pltpu.VMEM((V * KB, depth, BY + 16, width), jnp.float32),
            pltpu.VMEM((V, depth, padded, width), jnp.float32),
            pltpu.VMEM((ITERS, depth + 2 * W, padded, width), jnp.float32),
            pltpu.VMEM((depth, height, width), jnp.float32),
            pltpu.VMEM((V, 2 * CX, CX), jnp.bfloat16),
            pltpu.VMEM((V, CX, CX), jnp.bfloat16),
            pltpu.VMEM((V, 8, CX), jnp.float32),
            [
                pltpu.VMEM((ITERS, halo_planes[dz], halo_rows[db], width), jnp.bfloat16)
                for dz, db in DIRECTIONS
            ],
            [
                pltpu.VMEM((ITERS, halo_planes[dz], return_rows[db], width), jnp.float32)
                for dz, db in DIRECTIONS
            ],
            pltpu.SemaphoreType.DMA((bricks,)),
            pltpu.SemaphoreType.DMA((bricks,)),
            pltpu.SemaphoreType.DMA((bricks,)),
            pltpu.SemaphoreType.DMA((ITERS, count)),
            pltpu.SemaphoreType.DMA((ITERS, count)),
            pltpu.SemaphoreType.DMA((ITERS, count)),
            pltpu.SemaphoreType.DMA((ITERS, count)),
        ],
        compiler_params=pltpu.CompilerParams(
            collective_id=0, has_side_effects=True, vmem_limit_bytes=48 * 2**20
        ),
    )(routes, offsets, depth_taps, row_taps, column_taps, background, estimate, stored)


def solution(mesh):
    placed = (
        P("slab", "brick", None),
        P("brick", None, None, "slab", None, None),
        P(),
        P(),
        P(),
        P(),
        P(),
        P(),
    )
    return jax.shard_map(
        functools.partial(local, mesh.shape["slab"], mesh.shape["brick"]),
        mesh=mesh,
        in_specs=placed,
        out_specs=P("slab", "brick", None),
        check_vma=False,
    )
```

```python
import functools

import jax
import jax.numpy as jnp
from jax import lax
from jax.experimental import pallas as pl
from jax.experimental.pallas import tpu as pltpu
from jax.sharding import PartitionSpec as P

V = 6
CX = 128
BY = 16
KB = 4
W = 4
RY = 2
RX = 4
ITERS = 2
TZ = 2 * W + 1
TY = 2 * RY + 1
TX = 2 * RX + 1
MIDDLE = 1.25
SCALE = 43680.0
DIRECTIONS = [(dz, db) for dz in (-1, 0, 1) for db in (-1, 0, 1) if (dz, db) != (0, 0)]
MESH = pl.DeviceIdType.MESH


def kernel(
    slabs,
    bricks,
    routes_in,
    offsets_in,
    depth_in,
    row_in,
    column_in,
    background_in,
    estimate_in,
    stored,
    restored,
    routes,
    offsets,
    depth_taps,
    row_taps,
    column_taps,
    background,
    estimate,
    small_sem,
    staged,
    coded,
    received,
    slots,
    rounded,
    extended,
    zblur,
    level,
    back,
    spread,
    correction,
    total,
    forward,
    backward,
    scales,
    halos,
    returns,
    load_sem,
    data_send,
    data_recv,
    halo_send,
    halo_recv,
    return_send,
    return_recv,
):
    slab = lax.axis_index("slab")
    brick = lax.axis_index("brick")
    capacity = stored.shape[1]
    depth, height, _ = estimate.shape
    padded = height + 2 * W
    tiles = padded // 8

    def load_copy(target):
        return pltpu.make_async_copy(stored.at[target], staged.at[target], load_sem.at[target])

    small = [
        pltpu.make_async_copy(source, target, small_sem.at[index])
        for index, (source, target) in enumerate(
            [
                (estimate_in, estimate),
                (routes_in, routes),
                (offsets_in, offsets),
                (depth_in, depth_taps),
                (row_in, row_taps),
                (column_in, column_taps),
                (background_in, background),
            ]
        )
    ]
    for copy in small:
        copy.start()
    for step in range(1, bricks + 1):
        load_copy(lax.rem(brick + step, bricks)).start()

    def present(dz, db):
        there_slab = slab + dz
        there_brick = brick + db
        return (
            (there_slab >= 0) & (there_slab < slabs) & (there_brick >= 0) & (there_brick < bricks)
        )

    for buffer in tuple(halos) + tuple(returns):
        buffer[...] = jnp.zeros_like(buffer)

    barrier = pltpu.get_barrier_semaphore()
    for step in range(1, bricks):
        pl.semaphore_signal(
            barrier,
            inc=1,
            device_id=(slab, lax.rem(brick + step, bricks)),
            device_id_type=MESH,
        )
    expected = jnp.int32(bricks - 1)
    for dz, db in DIRECTIONS:
        if dz == 0:
            continue

        @pl.when(present(dz, db))
        def _():
            pl.semaphore_signal(
                barrier, inc=1, device_id=(slab + dz, brick + db), device_id_type=MESH
            )

        expected = expected + present(dz, db).astype(jnp.int32)
    small[0].wait()
    estimate_now = estimate[...]
    rounded[0] = estimate_now.astype(jnp.bfloat16)
    pl.semaphore_wait(barrier, expected)

    def halo_copy(sweep, index):
        dz, db = DIRECTIONS[index]
        planes = {-1: pl.ds(0, W), 0: pl.ds(0, depth), 1: pl.ds(depth - W, W)}[dz]
        rows = {-1: pl.ds(0, 16), 0: pl.ds(0, height), 1: pl.ds(height - 16, 16)}[db]
        return pltpu.make_async_remote_copy(
            src_ref=rounded.at[sweep, planes, rows],
            dst_ref=halos[index].at[sweep],
            send_sem=halo_send.at[sweep, index],
            recv_sem=halo_recv.at[sweep, index],
            device_id=(slab + dz, brick + db),
            device_id_type=MESH,
        )

    def return_copy(sweep, index):
        dz, db = DIRECTIONS[index]
        planes = {-1: pl.ds(0, W), 0: pl.ds(W, depth), 1: pl.ds(depth + W, W)}[dz]
        rows = {-1: pl.ds(0, 8), 0: pl.ds(0, padded), 1: pl.ds(padded - 8, 8)}[db]
        return pltpu.make_async_remote_copy(
            src_ref=correction.at[sweep, planes, rows],
            dst_ref=returns[index].at[sweep],
            send_sem=return_send.at[sweep, index],
            recv_sem=return_recv.at[sweep, index],
            device_id=(slab + dz, brick + db),
            device_id_type=MESH,
        )

    def send_all(copy, sweep):
        for index, (dz, db) in enumerate(DIRECTIONS):

            @pl.when(present(dz, db))
            def _():
                copy(sweep, index).start()

    def receive_all(copy, sweep):
        for index, (dz, db) in enumerate(DIRECTIONS):

            @pl.when(present(-dz, -db))
            def _():
                copy(sweep, index).wait_recv()

    def sent_all(copy, sweep):
        for index, (dz, db) in enumerate(DIRECTIONS):

            @pl.when(present(dz, db))
            def _():
                copy(sweep, index).wait_send()

    def data_copy(target, source):
        return pltpu.make_async_remote_copy(
            src_ref=coded.at[target],
            dst_ref=received.at[brick],
            send_sem=data_send.at[target],
            recv_sem=data_recv.at[source],
            device_id=(slab, target),
            device_id_type=MESH,
        )

    def encode(cells):
        return jnp.round((cells - MIDDLE) * SCALE).astype(jnp.int32).astype(jnp.int16)

    send_all(halo_copy, 0)

    def send_step(step, carry):
        target = lax.rem(brick + step, bricks)
        load_copy(target).wait()

        def code_slot(slot, inner):
            coded[target, slot] = encode(staged[target, slot])
            return inner

        lax.fori_loop(0, capacity, code_slot, 0)
        data_copy(target, brick).start()
        return carry

    lax.fori_loop(1, bricks, send_step, 0)
    load_copy(brick).wait()

    def code_own(slot, carry):
        received[brick, slot] = encode(staged[brick, slot])
        return carry

    lax.fori_loop(0, capacity, code_own, 0)

    for copy in small[1:]:
        copy.wait()

    def number_slots(position, carry):
        owner = routes[brick, position]
        count = jnp.int32(0)
        for other in range(V * KB):
            same = (routes[brick, other] == owner) & (other < position)
            count = count + jnp.where(same, 1, 0)
        slots[position] = jnp.minimum(count, capacity - 1)
        return carry

    lax.fori_loop(0, V * KB, number_slots, 0)

    row_index = lax.broadcasted_iota(jnp.int32, (CX, CX), 0)
    col_index = lax.broadcasted_iota(jnp.int32, (CX, CX), 1)

    def build_view(view, carry):
        sum_x = column_taps[view, 0]
        for position in range(1, TX):
            sum_x = sum_x + column_taps[view, position]
        sum_y = row_taps[view, 0]
        for position in range(1, TY):
            sum_y = sum_y + row_taps[view, position]
        sum_z = depth_taps[view, 0]
        for position in range(1, TZ):
            sum_z = sum_z + depth_taps[view, position]
        ones = jnp.ones((8, CX), jnp.float32)
        scales[view] = ones / (ones * (sum_y * sum_z))
        lag = row_index - col_index + RX
        matrix = jnp.zeros((CX, CX), jnp.float32)
        flipped = jnp.zeros((CX, CX), jnp.float32)
        bottom = jnp.full((1, CX), sum_x, jnp.float32)
        for position in range(TX):
            tap = jnp.full((1, CX), column_taps[view, position], jnp.float32) / bottom
            matrix = jnp.where(lag == position, tap, matrix)
            flipped = jnp.where(lag == 2 * RX - position, tap, flipped)
        matrix = matrix.astype(jnp.bfloat16)
        forward[view, 0:CX] = matrix
        forward[view, CX : 2 * CX] = matrix
        backward[view] = flipped.astype(jnp.bfloat16)
        return carry

    lax.fori_loop(0, V, build_view, 0)

    def clear(position, carry):
        back[position, :, 0:8] = jnp.zeros((depth, 8, CX), jnp.float32)
        back[position, :, 8 + BY : 16 + BY] = jnp.zeros((depth, 8, CX), jnp.float32)
        return carry

    lax.fori_loop(0, V * KB, clear, 0)

    for sweep in range(ITERS):
        if sweep > 0:
            rounded[sweep] = estimate_now.astype(jnp.bfloat16)
            send_all(halo_copy, sweep)
        extended[W : W + depth, W : W + height] = rounded[sweep].astype(jnp.float32)
        receive_all(halo_copy, sweep)
        for index, (dz, db) in enumerate(DIRECTIONS):
            planes = {1: (0, W), 0: (W, W + depth), -1: (W + depth, 2 * W + depth)}[dz]
            rows = {1: (0, W), 0: (W, W + height), -1: (W + height, padded)}[db]
            taken = {1: (16 - W, 16), 0: (0, height), -1: (0, W)}[db]
            block = halos[index][sweep].astype(jnp.float32)
            extended[planes[0] : planes[1], rows[0] : rows[1]] = block[:, taken[0] : taken[1]]

        def blur_tile(tile, carry):
            start = pl.multiple_of(tile * 8, 8)
            planes = [extended[z, pl.ds(start, 8)] for z in range(depth + 2 * W)]
            for view in range(V):
                taps = [depth_taps[view, position] for position in range(TZ)]
                for z in range(depth):
                    value = taps[0] * planes[z]
                    for position in range(1, TZ):
                        value = value + taps[position] * planes[z + position]
                    zblur[view, z, pl.ds(start, 8)] = value
            return carry

        lax.fori_loop(0, tiles, blur_tile, 0)

        def forward_view(view, carry):
            parts = []
            for piece in range(KB):
                first = piece * BY + W - RY + offsets[view, brick * KB + piece]
                part = row_taps[view, 0] * zblur[view, :, pl.ds(first, BY)]
                for tap in range(1, TY):
                    part = part + row_taps[view, tap] * zblur[view, :, pl.ds(first + tap, BY)]
                parts.append(part.reshape(depth * BY, CX))
            blurred = jnp.concatenate(parts, axis=0)
            high = blurred.astype(jnp.bfloat16)
            low = (blurred - high.astype(jnp.float32)).astype(jnp.bfloat16)
            blurred = jnp.dot(
                jnp.concatenate([high, low], axis=1),
                forward[view],
                preferred_element_type=jnp.float32,
            )
            level[view] = background[view] + scales[view, 0:1] * blurred
            return carry

        lax.fori_loop(0, V, forward_view, 0)

        if sweep == 0:

            def receive_step(step, carry):
                source = lax.rem(brick + step, bricks)
                data_copy(source, source).wait_recv()
                return carry

            lax.fori_loop(1, bricks, receive_step, 0)

        def backward_view(view, carry):
            codes = []
            for piece in range(KB):
                position = view * KB + piece
                code = received[routes[brick, position], slots[position]].astype(jnp.int32)
                codes.append(code.astype(jnp.float32).reshape(depth * BY, CX))
            data = jnp.concatenate(codes, axis=0) * (1.0 / SCALE) + MIDDLE
            ratio = data / level[view]
            result = scales[view, 0:1] * jnp.dot(
                ratio.astype(jnp.bfloat16), backward[view], preferred_element_type=jnp.float32
            )
            result = result.reshape(KB, depth, BY, CX)
            for piece in range(KB):
                back[view * KB + piece, :, 8 : 8 + BY] = result[piece]
            return carry

        lax.fori_loop(0, V, backward_view, 0)

        def spread_view(view, carry):
            edge = None
            for piece in range(KB):
                position = view * KB + piece
                shift = offsets[view, brick * KB + piece]
                value = None
                for tap in range(TY):
                    term = row_taps[view, tap] * back[
                        position, :, pl.ds(W - shift - (tap - RY), BY + 2 * W)
                    ]
                    value = term if value is None else value + term
                top = value[:, 0:8]
                if edge is not None:
                    top = top + edge
                spread[view, :, piece * BY : piece * BY + 8] = top
                spread[view, :, piece * BY + 8 : piece * BY + 16] = value[:, 8:16]
                edge = value[:, 16:24]
            spread[view, :, KB * BY : KB * BY + 8] = edge
            return carry

        lax.fori_loop(0, V, spread_view, 0)

        def deep_tile(tile, carry):
            start = pl.multiple_of(tile * 8, 8)
            sums = [None] * (depth + 2 * W)
            for view in range(V):
                taps = [depth_taps[view, position] for position in range(TZ)]
                for z in range(depth):
                    plane = spread[view, z, pl.ds(start, 8)]
                    for position in range(TZ):
                        term = taps[position] * plane
                        old = sums[z + position]
                        sums[z + position] = term if old is None else old + term
            for z in range(depth + 2 * W):
                correction[sweep, z, pl.ds(start, 8)] = sums[z]
            return carry

        lax.fori_loop(0, tiles, deep_tile, 0)

        send_all(return_copy, sweep)
        total[...] = correction[sweep, W : W + depth, W : W + height]
        receive_all(return_copy, sweep)
        for index, (dz, db) in enumerate(DIRECTIONS):
            planes = {1: (0, W), 0: (0, depth), -1: (depth - W, depth)}[dz]
            rows = {1: (0, W), 0: (0, height), -1: (height - W, height)}[db]
            taken = {1: (8 - W, 8), 0: (W, W + height), -1: (0, W)}[db]
            total[planes[0] : planes[1], rows[0] : rows[1]] += returns[index][
                sweep, :, taken[0] : taken[1]
            ]
        if sweep + 1 < ITERS:
            estimate_now = estimate_now * (total[...] / V)
        else:
            restored[...] = estimate_now * (total[...] / V)

    for sweep in range(ITERS):
        sent_all(halo_copy, sweep)
        sent_all(return_copy, sweep)

    def sent_step(step, carry):
        data_copy(lax.rem(brick + step, bricks), brick).wait_send()
        return carry

    lax.fori_loop(1, bricks, sent_step, 0)


def local(slabs, bricks, estimate, stored_data, routes, offsets, depth_taps, row_taps, column_taps, background):
    depth, height, width = estimate.shape
    stored = stored_data.reshape(stored_data.shape[1:])
    capacity = stored.shape[1]
    padded = height + 2 * W
    halo_planes = {-1: W, 0: depth, 1: W}
    halo_rows = {-1: 16, 0: height, 1: 16}
    return_rows = {-1: 8, 0: padded, 1: 8}
    anywhere = pl.BlockSpec(memory_space=pl.ANY)
    count = len(DIRECTIONS)
    return pl.pallas_call(
        functools.partial(kernel, slabs, bricks),
        out_shape=jax.ShapeDtypeStruct((depth, height, width), jnp.float32),
        in_specs=[anywhere] * 8,
        out_specs=pl.BlockSpec(memory_space=pltpu.VMEM),
        scratch_shapes=[
            pltpu.SMEM(routes.shape, jnp.int32),
            pltpu.SMEM(offsets.shape, jnp.int32),
            pltpu.SMEM(depth_taps.shape, jnp.float32),
            pltpu.SMEM(row_taps.shape, jnp.float32),
            pltpu.SMEM(column_taps.shape, jnp.float32),
            pltpu.SMEM(background.shape, jnp.float32),
            pltpu.VMEM((depth, height, width), jnp.float32),
            pltpu.SemaphoreType.DMA((7,)),
            pltpu.VMEM((bricks, capacity, depth, BY, width), jnp.float32),
            pltpu.VMEM((bricks, capacity, depth, BY, width), jnp.int16),
            pltpu.VMEM((bricks, capacity, depth, BY, width), jnp.int16),
            pltpu.SMEM((V * KB,), jnp.int32),
            pltpu.VMEM((ITERS, depth, height, width), jnp.bfloat16),
            pltpu.VMEM((depth + 2 * W, padded, width), jnp.float32),
            pltpu.VMEM((V, depth, padded, width), jnp.float32),
            pltpu.VMEM((V, KB * depth * BY, width), jnp.float32),
            pltpu.VMEM((V * KB, depth, BY + 16, width), jnp.float32),
            pltpu.VMEM((V, depth, padded, width), jnp.float32),
            pltpu.VMEM((ITERS, depth + 2 * W, padded, width), jnp.float32),
            pltpu.VMEM((depth, height, width), jnp.float32),
            pltpu.VMEM((V, 2 * CX, CX), jnp.bfloat16),
            pltpu.VMEM((V, CX, CX), jnp.bfloat16),
            pltpu.VMEM((V, 8, CX), jnp.float32),
            [
                pltpu.VMEM((ITERS, halo_planes[dz], halo_rows[db], width), jnp.bfloat16)
                for dz, db in DIRECTIONS
            ],
            [
                pltpu.VMEM((ITERS, halo_planes[dz], return_rows[db], width), jnp.float32)
                for dz, db in DIRECTIONS
            ],
            pltpu.SemaphoreType.DMA((bricks,)),
            pltpu.SemaphoreType.DMA((bricks,)),
            pltpu.SemaphoreType.DMA((bricks,)),
            pltpu.SemaphoreType.DMA((ITERS, count)),
            pltpu.SemaphoreType.DMA((ITERS, count)),
            pltpu.SemaphoreType.DMA((ITERS, count)),
            pltpu.SemaphoreType.DMA((ITERS, count)),
        ],
        compiler_params=pltpu.CompilerParams(
            collective_id=0, has_side_effects=True, vmem_limit_bytes=62 * 2**20
        ),
    )(routes, offsets, depth_taps, row_taps, column_taps, background, estimate, stored)


def solution(mesh):
    placed = (
        P("slab", "brick", None),
        P("brick", None, None, "slab", None, None),
        P(),
        P(),
        P(),
        P(),
        P(),
        P(),
    )
    return jax.shard_map(
        functools.partial(local, mesh.shape["slab"], mesh.shape["brick"]),
        mesh=mesh,
        in_specs=placed,
        out_specs=P("slab", "brick", None),
        check_vma=False,
    )
```

```python
import functools

import jax
import jax.numpy as jnp
from jax import lax
from jax.experimental import pallas as pl
from jax.experimental.pallas import tpu as pltpu
from jax.sharding import PartitionSpec as P

V = 6
CX = 128
BY = 16
KB = 4
W = 4
RY = 2
RX = 4
ITERS = 2
TZ = 2 * W + 1
TY = 2 * RY + 1
TX = 2 * RX + 1
MIDDLE = 1.25
SCALE = 43680.0
ROOT_SCALE = 5900.0
ROOT_ZERO = 32768.0
DIRECTIONS = [(dz, db) for dz in (-1, 0, 1) for db in (-1, 0, 1) if (dz, db) != (0, 0)]
MESH = pl.DeviceIdType.MESH


def kernel(
    slabs,
    bricks,
    routes_in,
    offsets_in,
    depth_in,
    row_in,
    column_in,
    background_in,
    estimate_in,
    stored,
    restored,
    routes,
    offsets,
    depth_taps,
    row_taps,
    column_taps,
    background,
    estimate,
    small_sem,
    staged,
    coded,
    received,
    slots,
    extended,
    zblur,
    level,
    back,
    spread,
    correction,
    total,
    forward,
    backward,
    scales,
    halos,
    returns,
    halos_out,
    returns_out,
    load_sem,
    data_send,
    data_recv,
    halo_send,
    halo_recv,
    return_send,
    return_recv,
):
    slab = lax.axis_index("slab")
    brick = lax.axis_index("brick")
    capacity = stored.shape[1]
    depth, height, _ = estimate.shape
    padded = height + 2 * W
    tiles = padded // 8

    def load_copy(target):
        return pltpu.make_async_copy(stored.at[target], staged.at[target], load_sem.at[target])

    small = [
        pltpu.make_async_copy(source, target, small_sem.at[index])
        for index, (source, target) in enumerate(
            [
                (estimate_in, estimate),
                (routes_in, routes),
                (offsets_in, offsets),
                (depth_in, depth_taps),
                (row_in, row_taps),
                (column_in, column_taps),
                (background_in, background),
            ]
        )
    ]
    for copy in small:
        copy.start()
    for step in range(1, bricks + 1):
        load_copy(lax.rem(brick + step, bricks)).start()

    def present(dz, db):
        there_slab = slab + dz
        there_brick = brick + db
        return (
            (there_slab >= 0) & (there_slab < slabs) & (there_brick >= 0) & (there_brick < bricks)
        )

    for buffer in halos:
        buffer[...] = jnp.zeros_like(buffer)
    for buffer in returns:
        buffer[...] = jnp.full(buffer.shape, -int(ROOT_ZERO), jnp.int32).astype(jnp.int16)

    def pack_halos(sweep, cells):
        for index, (dz, db) in enumerate(DIRECTIONS):
            planes = {-1: (0, W), 0: (0, depth), 1: (depth - W, depth)}[dz]
            rows = {-1: (0, W), 0: (0, height), 1: (height - W, height)}[db]
            halos_out[index][sweep] = jnp.concatenate(
                [cells[z, rows[0] : rows[1]] for z in range(*planes)], axis=0
            ).astype(jnp.bfloat16)

    barrier = pltpu.get_barrier_semaphore()
    for step in range(1, bricks):
        pl.semaphore_signal(
            barrier,
            inc=1,
            device_id=(slab, lax.rem(brick + step, bricks)),
            device_id_type=MESH,
        )
    expected = jnp.int32(bricks - 1)
    for dz, db in DIRECTIONS:
        if dz == 0:
            continue

        @pl.when(present(dz, db))
        def _():
            pl.semaphore_signal(
                barrier, inc=1, device_id=(slab + dz, brick + db), device_id_type=MESH
            )

        expected = expected + present(dz, db).astype(jnp.int32)
    small[0].wait()
    estimate_now = estimate[...]
    pack_halos(0, estimate_now)
    pl.semaphore_wait(barrier, expected)

    def halo_copy(sweep, index):
        dz, db = DIRECTIONS[index]
        return pltpu.make_async_remote_copy(
            src_ref=halos_out[index].at[sweep],
            dst_ref=halos[index].at[sweep],
            send_sem=halo_send.at[sweep, index],
            recv_sem=halo_recv.at[sweep, index],
            device_id=(slab + dz, brick + db),
            device_id_type=MESH,
        )

    def return_copy(sweep, index):
        dz, db = DIRECTIONS[index]
        return pltpu.make_async_remote_copy(
            src_ref=returns_out[index].at[sweep],
            dst_ref=returns[index].at[sweep],
            send_sem=return_send.at[sweep, index],
            recv_sem=return_recv.at[sweep, index],
            device_id=(slab + dz, brick + db),
            device_id_type=MESH,
        )

    def pack_returns(sweep):
        for index, (dz, db) in enumerate(DIRECTIONS):
            planes = {-1: (0, W), 0: (W, W + depth), 1: (W + depth, 2 * W + depth)}[dz]
            rows = {-1: (0, W), 0: (W, W + height), 1: (W + height, padded)}[db]
            piece = jnp.concatenate(
                [correction[sweep, z, rows[0] : rows[1]] for z in range(*planes)], axis=0
            )
            root = jnp.sqrt(jnp.maximum(piece, 1e-12))
            code = jnp.round(root * ROOT_SCALE - ROOT_ZERO).astype(jnp.int32)
            returns_out[index][sweep] = code.astype(jnp.int16)

    def send_all(copy, sweep):
        for index, (dz, db) in enumerate(DIRECTIONS):

            @pl.when(present(dz, db))
            def _():
                copy(sweep, index).start()

    def receive_all(copy, sweep):
        for index, (dz, db) in enumerate(DIRECTIONS):

            @pl.when(present(-dz, -db))
            def _():
                copy(sweep, index).wait_recv()

    def sent_all(copy, sweep):
        for index, (dz, db) in enumerate(DIRECTIONS):

            @pl.when(present(dz, db))
            def _():
                copy(sweep, index).wait_send()

    def data_copy(target, source):
        return pltpu.make_async_remote_copy(
            src_ref=coded.at[target],
            dst_ref=received.at[brick],
            send_sem=data_send.at[target],
            recv_sem=data_recv.at[source],
            device_id=(slab, target),
            device_id_type=MESH,
        )

    def encode(cells):
        return jnp.round((cells - MIDDLE) * SCALE).astype(jnp.int32).astype(jnp.int16)

    send_all(halo_copy, 0)

    def send_step(step, carry):
        target = lax.rem(brick + step, bricks)
        load_copy(target).wait()

        def code_slot(slot, inner):
            coded[target, slot] = encode(staged[target, slot])
            return inner

        lax.fori_loop(0, capacity, code_slot, 0)
        data_copy(target, brick).start()
        return carry

    lax.fori_loop(1, bricks, send_step, 0)
    load_copy(brick).wait()

    def code_own(slot, carry):
        received[brick, slot] = encode(staged[brick, slot])
        return carry

    lax.fori_loop(0, capacity, code_own, 0)

    for copy in small[1:]:
        copy.wait()

    def number_slots(position, carry):
        owner = routes[brick, position]
        count = jnp.int32(0)
        for other in range(V * KB):
            same = (routes[brick, other] == owner) & (other < position)
            count = count + jnp.where(same, 1, 0)
        slots[position] = jnp.minimum(count, capacity - 1)
        return carry

    lax.fori_loop(0, V * KB, number_slots, 0)

    row_index = lax.broadcasted_iota(jnp.int32, (CX, CX), 0)
    col_index = lax.broadcasted_iota(jnp.int32, (CX, CX), 1)

    def build_view(view, carry):
        sum_x = column_taps[view, 0]
        for position in range(1, TX):
            sum_x = sum_x + column_taps[view, position]
        sum_y = row_taps[view, 0]
        for position in range(1, TY):
            sum_y = sum_y + row_taps[view, position]
        sum_z = depth_taps[view, 0]
        for position in range(1, TZ):
            sum_z = sum_z + depth_taps[view, position]
        ones = jnp.ones((8, CX), jnp.float32)
        scales[view] = ones / (ones * (sum_y * sum_z))
        lag = row_index - col_index + RX
        matrix = jnp.zeros((CX, CX), jnp.float32)
        flipped = jnp.zeros((CX, CX), jnp.float32)
        bottom = jnp.full((1, CX), sum_x, jnp.float32)
        for position in range(TX):
            tap = jnp.full((1, CX), column_taps[view, position], jnp.float32) / bottom
            matrix = jnp.where(lag == position, tap, matrix)
            flipped = jnp.where(lag == 2 * RX - position, tap, flipped)
        matrix = matrix.astype(jnp.bfloat16)
        forward[view, 0:CX] = matrix
        forward[view, CX : 2 * CX] = matrix
        backward[view] = flipped.astype(jnp.bfloat16)
        return carry

    lax.fori_loop(0, V, build_view, 0)

    def clear(position, carry):
        back[position, :, 0:8] = jnp.zeros((depth, 8, CX), jnp.float32)
        back[position, :, 8 + BY : 16 + BY] = jnp.zeros((depth, 8, CX), jnp.float32)
        return carry

    lax.fori_loop(0, V * KB, clear, 0)

    for sweep in range(ITERS):
        if sweep > 0:
            pack_halos(sweep, estimate_now)
            send_all(halo_copy, sweep)
        extended[W : W + depth, W : W + height] = estimate_now.astype(jnp.bfloat16).astype(
            jnp.float32
        )
        receive_all(halo_copy, sweep)
        for index, (dz, db) in enumerate(DIRECTIONS):
            planes = {1: (0, W), 0: (W, W + depth), -1: (W + depth, 2 * W + depth)}[dz]
            rows = {1: (0, W), 0: (W, W + height), -1: (W + height, padded)}[db]
            block = halos[index][sweep].astype(jnp.float32)
            size = rows[1] - rows[0]
            for place, z in enumerate(range(*planes)):
                extended[z, rows[0] : rows[1]] = block[place * size : (place + 1) * size]

        def blur_tile(tile, carry):
            start = pl.multiple_of(tile * 8, 8)
            planes = [extended[z, pl.ds(start, 8)] for z in range(depth + 2 * W)]
            for view in range(V):
                taps = [depth_taps[view, position] for position in range(TZ)]
                for z in range(depth):
                    value = taps[0] * planes[z]
                    for position in range(1, TZ):
                        value = value + taps[position] * planes[z + position]
                    zblur[view, z, pl.ds(start, 8)] = value
            return carry

        lax.fori_loop(0, tiles, blur_tile, 0)

        def forward_view(view, carry):
            parts = []
            for piece in range(KB):
                first = piece * BY + W - RY + offsets[view, brick * KB + piece]
                part = row_taps[view, 0] * zblur[view, :, pl.ds(first, BY)]
                for tap in range(1, TY):
                    part = part + row_taps[view, tap] * zblur[view, :, pl.ds(first + tap, BY)]
                parts.append(part.reshape(depth * BY, CX))
            blurred = jnp.concatenate(parts, axis=0)
            high = blurred.astype(jnp.bfloat16)
            low = (blurred - high.astype(jnp.float32)).astype(jnp.bfloat16)
            blurred = jnp.dot(
                jnp.concatenate([high, low], axis=1),
                forward[view],
                preferred_element_type=jnp.float32,
            )
            level[view] = background[view] + scales[view, 0:1] * blurred
            return carry

        lax.fori_loop(0, V, forward_view, 0)

        if sweep == 0:

            def receive_step(step, carry):
                source = lax.rem(brick + step, bricks)
                data_copy(source, source).wait_recv()
                return carry

            lax.fori_loop(1, bricks, receive_step, 0)

        def backward_view(view, carry):
            codes = []
            for piece in range(KB):
                position = view * KB + piece
                code = received[routes[brick, position], slots[position]].astype(jnp.int32)
                codes.append(code.astype(jnp.float32).reshape(depth * BY, CX))
            data = jnp.concatenate(codes, axis=0) * (1.0 / SCALE) + MIDDLE
            ratio = data / level[view]
            result = scales[view, 0:1] * jnp.dot(
                ratio.astype(jnp.bfloat16), backward[view], preferred_element_type=jnp.float32
            )
            result = result.reshape(KB, depth, BY, CX)
            for piece in range(KB):
                back[view * KB + piece, :, 8 : 8 + BY] = result[piece]
            return carry

        lax.fori_loop(0, V, backward_view, 0)

        def spread_view(view, carry):
            edge = None
            for piece in range(KB):
                position = view * KB + piece
                shift = offsets[view, brick * KB + piece]
                value = None
                for tap in range(TY):
                    term = row_taps[view, tap] * back[
                        position, :, pl.ds(W - shift - (tap - RY), BY + 2 * W)
                    ]
                    value = term if value is None else value + term
                top = value[:, 0:8]
                if edge is not None:
                    top = top + edge
                spread[view, :, piece * BY : piece * BY + 8] = top
                spread[view, :, piece * BY + 8 : piece * BY + 16] = value[:, 8:16]
                edge = value[:, 16:24]
            spread[view, :, KB * BY : KB * BY + 8] = edge
            return carry

        lax.fori_loop(0, V, spread_view, 0)

        def deep_tile(tile, carry):
            start = pl.multiple_of(tile * 8, 8)
            sums = [None] * (depth + 2 * W)
            for view in range(V):
                taps = [depth_taps[view, position] for position in range(TZ)]
                for z in range(depth):
                    plane = spread[view, z, pl.ds(start, 8)]
                    for position in range(TZ):
                        term = taps[position] * plane
                        old = sums[z + position]
                        sums[z + position] = term if old is None else old + term
            for z in range(depth + 2 * W):
                correction[sweep, z, pl.ds(start, 8)] = sums[z]
            return carry

        lax.fori_loop(0, tiles, deep_tile, 0)

        pack_returns(sweep)
        send_all(return_copy, sweep)
        total[...] = correction[sweep, W : W + depth, W : W + height]
        receive_all(return_copy, sweep)
        for index, (dz, db) in enumerate(DIRECTIONS):
            planes = {1: (0, W), 0: (0, depth), -1: (depth - W, depth)}[dz]
            rows = {1: (0, W), 0: (0, height), -1: (height - W, height)}[db]
            code = returns[index][sweep].astype(jnp.int32).astype(jnp.float32)
            root = (code + ROOT_ZERO) * (1.0 / ROOT_SCALE)
            piece = root * root
            size = rows[1] - rows[0]
            for place, z in enumerate(range(*planes)):
                total[z, rows[0] : rows[1]] += piece[place * size : (place + 1) * size]
        if sweep + 1 < ITERS:
            estimate_now = estimate_now * (total[...] / V)
        else:
            restored[...] = estimate_now * (total[...] / V)

    for sweep in range(ITERS):
        sent_all(halo_copy, sweep)
        sent_all(return_copy, sweep)

    def sent_step(step, carry):
        data_copy(lax.rem(brick + step, bricks), brick).wait_send()
        return carry

    lax.fori_loop(1, bricks, sent_step, 0)


def local(slabs, bricks, estimate, stored_data, routes, offsets, depth_taps, row_taps, column_taps, background):
    depth, height, width = estimate.shape
    stored = stored_data.reshape(stored_data.shape[1:])
    capacity = stored.shape[1]
    padded = height + 2 * W
    halo_planes = {-1: W, 0: depth, 1: W}
    halo_rows = {-1: W, 0: height, 1: W}

    def faces(dtype):
        return [
            pltpu.VMEM((ITERS, halo_planes[dz] * halo_rows[db], width), dtype)
            for dz, db in DIRECTIONS
        ]

    anywhere = pl.BlockSpec(memory_space=pl.ANY)
    count = len(DIRECTIONS)
    return pl.pallas_call(
        functools.partial(kernel, slabs, bricks),
        out_shape=jax.ShapeDtypeStruct((depth, height, width), jnp.float32),
        in_specs=[anywhere] * 8,
        out_specs=pl.BlockSpec(memory_space=pltpu.VMEM),
        scratch_shapes=[
            pltpu.SMEM(routes.shape, jnp.int32),
            pltpu.SMEM(offsets.shape, jnp.int32),
            pltpu.SMEM(depth_taps.shape, jnp.float32),
            pltpu.SMEM(row_taps.shape, jnp.float32),
            pltpu.SMEM(column_taps.shape, jnp.float32),
            pltpu.SMEM(background.shape, jnp.float32),
            pltpu.VMEM((depth, height, width), jnp.float32),
            pltpu.SemaphoreType.DMA((7,)),
            pltpu.VMEM((bricks, capacity, depth, BY, width), jnp.float32),
            pltpu.VMEM((bricks, capacity, depth, BY, width), jnp.int16),
            pltpu.VMEM((bricks, capacity, depth, BY, width), jnp.int16),
            pltpu.SMEM((V * KB,), jnp.int32),
            pltpu.VMEM((depth + 2 * W, padded, width), jnp.float32),
            pltpu.VMEM((V, depth, padded, width), jnp.float32),
            pltpu.VMEM((V, KB * depth * BY, width), jnp.float32),
            pltpu.VMEM((V * KB, depth, BY + 16, width), jnp.float32),
            pltpu.VMEM((V, depth, padded, width), jnp.float32),
            pltpu.VMEM((ITERS, depth + 2 * W, padded, width), jnp.float32),
            pltpu.VMEM((depth, height, width), jnp.float32),
            pltpu.VMEM((V, 2 * CX, CX), jnp.bfloat16),
            pltpu.VMEM((V, CX, CX), jnp.bfloat16),
            pltpu.VMEM((V, 8, CX), jnp.float32),
            faces(jnp.bfloat16),
            faces(jnp.int16),
            faces(jnp.bfloat16),
            faces(jnp.int16),
            pltpu.SemaphoreType.DMA((bricks,)),
            pltpu.SemaphoreType.DMA((bricks,)),
            pltpu.SemaphoreType.DMA((bricks,)),
            pltpu.SemaphoreType.DMA((ITERS, count)),
            pltpu.SemaphoreType.DMA((ITERS, count)),
            pltpu.SemaphoreType.DMA((ITERS, count)),
            pltpu.SemaphoreType.DMA((ITERS, count)),
        ],
        compiler_params=pltpu.CompilerParams(
            collective_id=0, has_side_effects=True, vmem_limit_bytes=62 * 2**20
        ),
    )(routes, offsets, depth_taps, row_taps, column_taps, background, estimate, stored)


def solution(mesh):
    placed = (
        P("slab", "brick", None),
        P("brick", None, None, "slab", None, None),
        P(),
        P(),
        P(),
        P(),
        P(),
        P(),
    )
    return jax.shard_map(
        functools.partial(local, mesh.shape["slab"], mesh.shape["brick"]),
        mesh=mesh,
        in_specs=placed,
        out_specs=P("slab", "brick", None),
        check_vma=False,
    )
```

```python
import functools

import jax
import jax.numpy as jnp
from jax import lax
from jax.experimental import pallas as pl
from jax.experimental.pallas import tpu as pltpu
from jax.sharding import PartitionSpec as P

V = 6
CX = 128
BY = 16
KB = 4
W = 4
RY = 2
RX = 4
ITERS = 2
TZ = 2 * W + 1
TY = 2 * RY + 1
TX = 2 * RX + 1
MIDDLE = 1.25
SCALE = 43680.0
ROOT_SCALE = 5900.0
ROOT_ZERO = 32768.0
DIRECTIONS = [(dz, db) for dz in (-1, 0, 1) for db in (-1, 0, 1) if (dz, db) != (0, 0)]
MESH = pl.DeviceIdType.MESH


def kernel(
    slabs,
    bricks,
    routes_in,
    offsets_in,
    depth_in,
    row_in,
    column_in,
    background_in,
    estimate_in,
    stored,
    restored,
    routes,
    offsets,
    depth_taps,
    row_taps,
    column_taps,
    background,
    estimate,
    small_sem,
    staged,
    coded,
    received,
    slots,
    extended,
    zblur,
    level,
    back,
    spread,
    correction,
    total,
    forward,
    backward,
    scales,
    halos,
    returns,
    halos_out,
    returns_out,
    load_sem,
    data_send,
    data_recv,
    halo_send,
    halo_recv,
    return_send,
    return_recv,
):
    slab = lax.axis_index("slab")
    brick = lax.axis_index("brick")
    capacity = stored.shape[1]
    depth, height, _ = estimate.shape
    padded = height + 2 * W
    tiles = padded // 8

    def load_copy(target):
        return pltpu.make_async_copy(stored.at[target], staged.at[target], load_sem.at[target])

    small = [
        pltpu.make_async_copy(source, target, small_sem.at[index])
        for index, (source, target) in enumerate(
            [
                (estimate_in, estimate),
                (routes_in, routes),
                (offsets_in, offsets),
                (depth_in, depth_taps),
                (row_in, row_taps),
                (column_in, column_taps),
                (background_in, background),
            ]
        )
    ]
    for copy in small:
        copy.start()
    wide = max(1, round((bricks // 2) ** 0.5))
    if wide * wide * 2 != bricks:
        wide = bricks // 2
    high_count = bricks // 2 // wide

    def partner(step):
        shift = bricks - 1 - step
        chip = brick // 2
        row = (chip // wide + shift // 2 // wide) % high_count
        column = (chip % wide + shift // 2 % wide) % wide
        return (row * wide + column) * 2 + (brick % 2 + shift % 2) % 2

    for step in range(bricks):
        load_copy(partner(step)).start()

    def present(dz, db):
        there_slab = slab + dz
        there_brick = brick + db
        return (
            (there_slab >= 0) & (there_slab < slabs) & (there_brick >= 0) & (there_brick < bricks)
        )

    for buffer in halos:
        buffer[...] = jnp.zeros_like(buffer)
    for buffer in returns:
        buffer[...] = jnp.full(buffer.shape, -int(ROOT_ZERO), jnp.int32).astype(jnp.int16)

    def pack_halos(sweep, cells):
        for index, (dz, db) in enumerate(DIRECTIONS):
            planes = {-1: (0, W), 0: (0, depth), 1: (depth - W, depth)}[dz]
            rows = {-1: (0, W), 0: (0, height), 1: (height - W, height)}[db]
            halos_out[index][sweep] = jnp.concatenate(
                [cells[z, rows[0] : rows[1]] for z in range(*planes)], axis=0
            ).astype(jnp.bfloat16)

    barrier = pltpu.get_barrier_semaphore()
    for step in range(1, bricks):
        pl.semaphore_signal(
            barrier,
            inc=1,
            device_id=(slab, lax.rem(brick + step, bricks)),
            device_id_type=MESH,
        )
    expected = jnp.int32(bricks - 1)
    for dz, db in DIRECTIONS:
        if dz == 0:
            continue

        @pl.when(present(dz, db))
        def _():
            pl.semaphore_signal(
                barrier, inc=1, device_id=(slab + dz, brick + db), device_id_type=MESH
            )

        expected = expected + present(dz, db).astype(jnp.int32)
    small[0].wait()
    estimate_now = estimate[...]
    pack_halos(0, estimate_now)

    def halo_copy(sweep, index):
        dz, db = DIRECTIONS[index]
        return pltpu.make_async_remote_copy(
            src_ref=halos_out[index].at[sweep],
            dst_ref=halos[index].at[sweep],
            send_sem=halo_send.at[sweep, index],
            recv_sem=halo_recv.at[sweep, index],
            device_id=(slab + dz, brick + db),
            device_id_type=MESH,
        )

    def return_copy(sweep, index):
        dz, db = DIRECTIONS[index]
        return pltpu.make_async_remote_copy(
            src_ref=returns_out[index].at[sweep],
            dst_ref=returns[index].at[sweep],
            send_sem=return_send.at[sweep, index],
            recv_sem=return_recv.at[sweep, index],
            device_id=(slab + dz, brick + db),
            device_id_type=MESH,
        )

    def pack_returns(sweep):
        for index, (dz, db) in enumerate(DIRECTIONS):
            planes = {-1: (0, W), 0: (W, W + depth), 1: (W + depth, 2 * W + depth)}[dz]
            rows = {-1: (0, W), 0: (W, W + height), 1: (W + height, padded)}[db]
            piece = jnp.concatenate(
                [correction[sweep, z, rows[0] : rows[1]] for z in range(*planes)], axis=0
            )
            root = jnp.sqrt(jnp.maximum(piece, 1e-12))
            code = jnp.round(root * ROOT_SCALE - ROOT_ZERO).astype(jnp.int32)
            returns_out[index][sweep] = code.astype(jnp.int16)

    def send_all(copy, sweep):
        for index, (dz, db) in enumerate(DIRECTIONS):

            @pl.when(present(dz, db))
            def _():
                copy(sweep, index).start()

    def receive_all(copy, sweep):
        for index, (dz, db) in enumerate(DIRECTIONS):

            @pl.when(present(-dz, -db))
            def _():
                copy(sweep, index).wait_recv()

    def sent_all(copy, sweep):
        for index, (dz, db) in enumerate(DIRECTIONS):

            @pl.when(present(dz, db))
            def _():
                copy(sweep, index).wait_send()

    def data_copy(target, source):
        return pltpu.make_async_remote_copy(
            src_ref=coded.at[target],
            dst_ref=received.at[brick],
            send_sem=data_send.at[target],
            recv_sem=data_recv.at[source],
            device_id=(slab, target),
            device_id_type=MESH,
        )

    def encode(cells):
        return jnp.round((cells - MIDDLE) * SCALE).astype(jnp.int32).astype(jnp.int16)

    def code_step(step, carry):
        target = partner(step)
        load_copy(target).wait()

        def code_slot(slot, inner):
            coded[target, slot] = encode(staged[target, slot])
            return inner

        lax.fori_loop(0, capacity, code_slot, 0)
        return carry

    lax.fori_loop(0, bricks - 1, code_step, 0)
    pl.semaphore_wait(barrier, expected)
    send_all(halo_copy, 0)
    for step in range(bricks - 1):
        data_copy(partner(step), brick).start()
    load_copy(brick).wait()

    def code_own(slot, carry):
        received[brick, slot] = encode(staged[brick, slot])
        return carry

    lax.fori_loop(0, capacity, code_own, 0)

    for copy in small[1:]:
        copy.wait()

    def number_slots(position, carry):
        owner = routes[brick, position]
        count = jnp.int32(0)
        for other in range(V * KB):
            same = (routes[brick, other] == owner) & (other < position)
            count = count + jnp.where(same, 1, 0)
        slots[position] = jnp.minimum(count, capacity - 1)
        return carry

    lax.fori_loop(0, V * KB, number_slots, 0)

    row_index = lax.broadcasted_iota(jnp.int32, (CX, CX), 0)
    col_index = lax.broadcasted_iota(jnp.int32, (CX, CX), 1)

    def build_view(view, carry):
        sum_x = column_taps[view, 0]
        for position in range(1, TX):
            sum_x = sum_x + column_taps[view, position]
        sum_y = row_taps[view, 0]
        for position in range(1, TY):
            sum_y = sum_y + row_taps[view, position]
        sum_z = depth_taps[view, 0]
        for position in range(1, TZ):
            sum_z = sum_z + depth_taps[view, position]
        ones = jnp.ones((8, CX), jnp.float32)
        scales[view] = ones / (ones * (sum_y * sum_z))
        lag = row_index - col_index + RX
        matrix = jnp.zeros((CX, CX), jnp.float32)
        flipped = jnp.zeros((CX, CX), jnp.float32)
        bottom = jnp.full((1, CX), sum_x, jnp.float32)
        for position in range(TX):
            tap = jnp.full((1, CX), column_taps[view, position], jnp.float32) / bottom
            matrix = jnp.where(lag == position, tap, matrix)
            flipped = jnp.where(lag == 2 * RX - position, tap, flipped)
        matrix = matrix.astype(jnp.bfloat16)
        forward[view, 0:CX] = matrix
        forward[view, CX : 2 * CX] = matrix
        backward[view] = flipped.astype(jnp.bfloat16)
        return carry

    lax.fori_loop(0, V, build_view, 0)

    def clear(position, carry):
        back[position, :, 0:8] = jnp.zeros((depth, 8, CX), jnp.float32)
        back[position, :, 8 + BY : 16 + BY] = jnp.zeros((depth, 8, CX), jnp.float32)
        return carry

    lax.fori_loop(0, V * KB, clear, 0)

    for sweep in range(ITERS):
        if sweep > 0:
            pack_halos(sweep, estimate_now)
            send_all(halo_copy, sweep)
        extended[W : W + depth, W : W + height] = estimate_now.astype(jnp.bfloat16).astype(
            jnp.float32
        )
        receive_all(halo_copy, sweep)
        for index, (dz, db) in enumerate(DIRECTIONS):
            planes = {1: (0, W), 0: (W, W + depth), -1: (W + depth, 2 * W + depth)}[dz]
            rows = {1: (0, W), 0: (W, W + height), -1: (W + height, padded)}[db]
            block = halos[index][sweep].astype(jnp.float32)
            size = rows[1] - rows[0]
            for place, z in enumerate(range(*planes)):
                extended[z, rows[0] : rows[1]] = block[place * size : (place + 1) * size]

        def blur_tile(tile, carry):
            start = pl.multiple_of(tile * 8, 8)
            planes = [extended[z, pl.ds(start, 8)] for z in range(depth + 2 * W)]
            for view in range(V):
                taps = [depth_taps[view, position] for position in range(TZ)]
                for z in range(depth):
                    value = taps[0] * planes[z]
                    for position in range(1, TZ):
                        value = value + taps[position] * planes[z + position]
                    zblur[view, z, pl.ds(start, 8)] = value
            return carry

        lax.fori_loop(0, tiles, blur_tile, 0)

        def forward_view(view, carry):
            parts = []
            for piece in range(KB):
                first = piece * BY + W - RY + offsets[view, brick * KB + piece]
                part = row_taps[view, 0] * zblur[view, :, pl.ds(first, BY)]
                for tap in range(1, TY):
                    part = part + row_taps[view, tap] * zblur[view, :, pl.ds(first + tap, BY)]
                parts.append(part.reshape(depth * BY, CX))
            blurred = jnp.concatenate(parts, axis=0)
            high = blurred.astype(jnp.bfloat16)
            low = (blurred - high.astype(jnp.float32)).astype(jnp.bfloat16)
            blurred = jnp.dot(
                jnp.concatenate([high, low], axis=1),
                forward[view],
                preferred_element_type=jnp.float32,
            )
            level[view] = background[view] + scales[view, 0:1] * blurred
            return carry

        lax.fori_loop(0, V, forward_view, 0)

        if sweep == 0:

            def receive_step(step, carry):
                source = lax.rem(brick + step, bricks)
                data_copy(source, source).wait_recv()
                return carry

            lax.fori_loop(1, bricks, receive_step, 0)

        def backward_view(view, carry):
            codes = []
            for piece in range(KB):
                position = view * KB + piece
                code = received[routes[brick, position], slots[position]].astype(jnp.int32)
                codes.append(code.astype(jnp.float32).reshape(depth * BY, CX))
            data = jnp.concatenate(codes, axis=0) * (1.0 / SCALE) + MIDDLE
            ratio = data / level[view]
            result = scales[view, 0:1] * jnp.dot(
                ratio.astype(jnp.bfloat16), backward[view], preferred_element_type=jnp.float32
            )
            result = result.reshape(KB, depth, BY, CX)
            for piece in range(KB):
                back[view * KB + piece, :, 8 : 8 + BY] = result[piece]
            return carry

        lax.fori_loop(0, V, backward_view, 0)

        def spread_view(view, carry):
            edge = None
            for piece in range(KB):
                position = view * KB + piece
                shift = offsets[view, brick * KB + piece]
                value = None
                for tap in range(TY):
                    term = row_taps[view, tap] * back[
                        position, :, pl.ds(W - shift - (tap - RY), BY + 2 * W)
                    ]
                    value = term if value is None else value + term
                top = value[:, 0:8]
                if edge is not None:
                    top = top + edge
                spread[view, :, piece * BY : piece * BY + 8] = top
                spread[view, :, piece * BY + 8 : piece * BY + 16] = value[:, 8:16]
                edge = value[:, 16:24]
            spread[view, :, KB * BY : KB * BY + 8] = edge
            return carry

        lax.fori_loop(0, V, spread_view, 0)

        def deep_tile(tile, carry):
            start = pl.multiple_of(tile * 8, 8)
            sums = [None] * (depth + 2 * W)
            for view in range(V):
                taps = [depth_taps[view, position] for position in range(TZ)]
                for z in range(depth):
                    plane = spread[view, z, pl.ds(start, 8)]
                    for position in range(TZ):
                        term = taps[position] * plane
                        old = sums[z + position]
                        sums[z + position] = term if old is None else old + term
            for z in range(depth + 2 * W):
                correction[sweep, z, pl.ds(start, 8)] = sums[z]
            return carry

        lax.fori_loop(0, tiles, deep_tile, 0)

        pack_returns(sweep)
        send_all(return_copy, sweep)
        total[...] = correction[sweep, W : W + depth, W : W + height]
        receive_all(return_copy, sweep)
        for index, (dz, db) in enumerate(DIRECTIONS):
            planes = {1: (0, W), 0: (0, depth), -1: (depth - W, depth)}[dz]
            rows = {1: (0, W), 0: (0, height), -1: (height - W, height)}[db]
            code = returns[index][sweep].astype(jnp.int32).astype(jnp.float32)
            root = (code + ROOT_ZERO) * (1.0 / ROOT_SCALE)
            piece = root * root
            size = rows[1] - rows[0]
            for place, z in enumerate(range(*planes)):
                total[z, rows[0] : rows[1]] += piece[place * size : (place + 1) * size]
        if sweep + 1 < ITERS:
            estimate_now = estimate_now * (total[...] / V)
        else:
            restored[...] = estimate_now * (total[...] / V)

    for sweep in range(ITERS):
        sent_all(halo_copy, sweep)
        sent_all(return_copy, sweep)

    def sent_step(step, carry):
        data_copy(lax.rem(brick + step, bricks), brick).wait_send()
        return carry

    lax.fori_loop(1, bricks, sent_step, 0)


def local(slabs, bricks, estimate, stored_data, routes, offsets, depth_taps, row_taps, column_taps, background):
    depth, height, width = estimate.shape
    stored = stored_data.reshape(stored_data.shape[1:])
    capacity = stored.shape[1]
    padded = height + 2 * W
    halo_planes = {-1: W, 0: depth, 1: W}
    halo_rows = {-1: W, 0: height, 1: W}

    def faces(dtype):
        return [
            pltpu.VMEM((ITERS, halo_planes[dz] * halo_rows[db], width), dtype)
            for dz, db in DIRECTIONS
        ]

    anywhere = pl.BlockSpec(memory_space=pl.ANY)
    count = len(DIRECTIONS)
    return pl.pallas_call(
        functools.partial(kernel, slabs, bricks),
        out_shape=jax.ShapeDtypeStruct((depth, height, width), jnp.float32),
        in_specs=[anywhere] * 8,
        out_specs=pl.BlockSpec(memory_space=pltpu.VMEM),
        scratch_shapes=[
            pltpu.SMEM(routes.shape, jnp.int32),
            pltpu.SMEM(offsets.shape, jnp.int32),
            pltpu.SMEM(depth_taps.shape, jnp.float32),
            pltpu.SMEM(row_taps.shape, jnp.float32),
            pltpu.SMEM(column_taps.shape, jnp.float32),
            pltpu.SMEM(background.shape, jnp.float32),
            pltpu.VMEM((depth, height, width), jnp.float32),
            pltpu.SemaphoreType.DMA((7,)),
            pltpu.VMEM((bricks, capacity, depth, BY, width), jnp.float32),
            pltpu.VMEM((bricks, capacity, depth, BY, width), jnp.int16),
            pltpu.VMEM((bricks, capacity, depth, BY, width), jnp.int16),
            pltpu.SMEM((V * KB,), jnp.int32),
            pltpu.VMEM((depth + 2 * W, padded, width), jnp.float32),
            pltpu.VMEM((V, depth, padded, width), jnp.float32),
            pltpu.VMEM((V, KB * depth * BY, width), jnp.float32),
            pltpu.VMEM((V * KB, depth, BY + 16, width), jnp.float32),
            pltpu.VMEM((V, depth, padded, width), jnp.float32),
            pltpu.VMEM((ITERS, depth + 2 * W, padded, width), jnp.float32),
            pltpu.VMEM((depth, height, width), jnp.float32),
            pltpu.VMEM((V, 2 * CX, CX), jnp.bfloat16),
            pltpu.VMEM((V, CX, CX), jnp.bfloat16),
            pltpu.VMEM((V, 8, CX), jnp.float32),
            faces(jnp.bfloat16),
            faces(jnp.int16),
            faces(jnp.bfloat16),
            faces(jnp.int16),
            pltpu.SemaphoreType.DMA((bricks,)),
            pltpu.SemaphoreType.DMA((bricks,)),
            pltpu.SemaphoreType.DMA((bricks,)),
            pltpu.SemaphoreType.DMA((ITERS, count)),
            pltpu.SemaphoreType.DMA((ITERS, count)),
            pltpu.SemaphoreType.DMA((ITERS, count)),
            pltpu.SemaphoreType.DMA((ITERS, count)),
        ],
        compiler_params=pltpu.CompilerParams(
            collective_id=0, has_side_effects=True, vmem_limit_bytes=62 * 2**20
        ),
    )(routes, offsets, depth_taps, row_taps, column_taps, background, estimate, stored)


def solution(mesh):
    placed = (
        P("slab", "brick", None),
        P("brick", None, None, "slab", None, None),
        P(),
        P(),
        P(),
        P(),
        P(),
        P(),
    )
    return jax.shard_map(
        functools.partial(local, mesh.shape["slab"], mesh.shape["brick"]),
        mesh=mesh,
        in_specs=placed,
        out_specs=P("slab", "brick", None),
        check_vma=False,
    )
```
